128 devices in a mesh: prompt: 8 (over z, core), learner: 16 (over x, y).
Axes of the slice: x: 4, y: 4, z: 4, core: 2. Of those that a mesh axis runs over, the one named last changes fastest.
Arguments:
- prefix_k: bfloat16 [8, 2048, 512], P('prompt', 'learner'), may hold values from -6 to 6
- prefix_v: bfloat16 [8, 2048, 512], P('prompt', 'learner'), may hold values from -30 to 30
- queries: bfloat16 [128, 256, 2560], P(('prompt', 'learner')), may hold values from -6 to 6
- comp_k: bfloat16 [128, 256, 512], P(('prompt', 'learner')), may hold values from -6 to 6
- comp_v: bfloat16 [128, 256, 512], P(('prompt', 'learner')), may hold values from -30 to 30
- out_grad: bfloat16 [128, 256, 2560], P(('prompt', 'learner')), may hold values from -6 to 6
- lengths: int32 [128], replicated, may hold values from 128 to 256, as said below
- owner_map: int32 [8], replicated, may hold values from 0 to 7, each once
Outputs:
- attended: bfloat16 [128, 256, 2560], P(('prompt', 'learner'))
- grad_queries: bfloat16 [128, 256, 2560], P(('prompt', 'learner'))
- grad_comp_k: bfloat16 [128, 256, 512], P(('prompt', 'learner'))
- grad_comp_v: bfloat16 [128, 256, 512], P(('prompt', 'learner'))
- grad_prefix_k: float32 [8, 2048, 512], P('prompt', 'learner')
- grad_prefix_v: float32 [8, 2048, 512], P('prompt', 'learner')
The draws below stay inside these ranges and needn't reach their ends.
Inputs may be any that keep to these rules, and one draw needn't show every extreme that they name: `lengths`: every length is a multiple of 128; among the 16 completions of each prompt one has length exactly 256. `owner_map`: a permutation of the prompt groups.
All inputs are finite; a program needn't handle non-finite values.
Results may differ from the reference program's by a relative error of at most 0.04.
Values may be sent and summed in bfloat16 or wider, within the bound.
No kernel may reach another device: no remote copies, remote signals or barrier semaphores. Data moves between devices by JAX's collectives and lax.ppermute only.
A program may use at most 192 MiB of HBM per device.

```python
import jax
import jax.numpy as jnp
from jax import lax

Q_HEADS = 20
KV_HEADS = 4
HEAD_DIM = 128
ROW_BLOCK = 128
PREFIX = 2048
COMP_LEN = 256
Q_PER_KV = 5
LEN_BLOCKS = 2
PROMPTS = 8
PER_PROMPT = 16
COMPLETIONS = 128


def draw_queries(key, part):
    key = jax.random.fold_in(key, 11)
    shape = (COMPLETIONS, COMP_LEN, Q_HEADS * HEAD_DIM)
    result = 1.5 * jnp.clip(jax.random.normal(key, shape, jnp.float32), -4.0, 4.0)
    return result.astype(jnp.bfloat16)


def draw_prefix_k(key, part):
    key = jax.random.fold_in(key, 23)
    shape = (PROMPTS, PREFIX, KV_HEADS * HEAD_DIM)
    result = jnp.clip(jax.random.normal(key, shape, jnp.float32), -4.0, 4.0)
    return result.astype(jnp.bfloat16)


def draw_lengths(key, part):
    key = jax.random.fold_in(key, 5)
    key_a, key_b = jax.random.split(key)
    blocks = jax.random.randint(key_a, (COMPLETIONS,), 1, LEN_BLOCKS + 1, dtype=jnp.int32)
    chosen = jax.random.randint(key_b, (COMPLETIONS // PER_PROMPT,), 0, PER_PROMPT, dtype=jnp.int32)
    comp_no = jnp.arange(COMPLETIONS, dtype=jnp.int32)
    forced = comp_no % PER_PROMPT == chosen[comp_no // PER_PROMPT]
    return (jnp.where(forced, LEN_BLOCKS, blocks) * ROW_BLOCK).astype(jnp.int32)


def steps_of(stream_key, extent, cuts, low, largest):
    loudness = 1.0
    for position, parts in cuts:
        draws = jax.random.uniform(jax.random.fold_in(jax.random.fold_in(stream_key, 6), position), (parts,), jnp.float32, low / len(cuts), largest / len(cuts))
        loudness = loudness * jnp.repeat(jnp.exp(draws), extent[position] // parts).reshape((-1,) + (1,) * (len(extent) - 1 - position))
    return loudness


def scatter_about(rng, shape, width, most, shards=(), kind=jnp.bfloat16):
    values = jax.random.normal(rng, shape, jnp.float32) * width
    if len(shards) > 0:
        values = steps_of(rng, shape, shards, -0.22, 0.18) * values
    return jnp.clip(values, min=-most, max=most).astype(kind)


def setup_inputs(seed: int = 0) -> dict:
    seeds = jax.random.split(jax.random.key(seed), 9)
    return {
        "prefix_k": draw_prefix_k(jax.random.fold_in(seeds[8], 71), 0),
        "prefix_v": scatter_about(seeds[1], (PROMPTS, PREFIX, KV_HEADS * HEAD_DIM), 6.0, 30.0, ((0, 8), (1, 16))),
        "queries": draw_queries(jax.random.fold_in(seeds[8], 71), 0),
        "comp_k": scatter_about(seeds[3], (COMPLETIONS, COMP_LEN, KV_HEADS * HEAD_DIM), 1.0, 6.0, ((0, 128),)),
        "comp_v": scatter_about(seeds[4], (COMPLETIONS, COMP_LEN, KV_HEADS * HEAD_DIM), 6.0, 30.0, ((0, 128),)),
        "out_grad": scatter_about(seeds[5], (COMPLETIONS, COMP_LEN, Q_HEADS * HEAD_DIM), 1.0, 6.0, ((0, 128),)),
        "lengths": draw_lengths(jax.random.fold_in(seeds[8], 71), 0),
        "owner_map": jax.random.permutation(seeds[7], PROMPTS).astype(jnp.int32),
    }


very_low = -1.0e30


def widen(array):
    return array.astype(jnp.float32)


def attend_one(query_rows, key_pre, value_pre, key_own, value_own, grad_rows, length):
    inv_root = HEAD_DIM ** -0.5
    highest = lax.Precision.HIGHEST
    query_f = widen(query_rows).reshape(COMP_LEN, KV_HEADS, Q_PER_KV, HEAD_DIM)
    pre_keys = widen(key_pre).reshape(PREFIX, KV_HEADS, HEAD_DIM)
    pre_vals = widen(value_pre).reshape(PREFIX, KV_HEADS, HEAD_DIM)
    own_keys = widen(key_own).reshape(COMP_LEN, KV_HEADS, HEAD_DIM)
    own_vals = widen(value_own).reshape(COMP_LEN, KV_HEADS, HEAD_DIM)
    grad_f = widen(grad_rows).reshape(COMP_LEN, KV_HEADS, Q_PER_KV, HEAD_DIM)
    positions = jnp.arange(COMP_LEN, dtype=jnp.int32)
    live_rows = positions < length
    visible = positions[None, :] <= positions[:, None]
    s_pre = jnp.einsum("ckgd,tkd->kgct", query_f, pre_keys, precision=highest) * inv_root
    s_own = jnp.einsum("ikgd,jkd->kgij", query_f, own_keys, precision=highest) * inv_root
    s_own = jnp.where(visible, s_own, very_low)
    row_top = jnp.maximum(jnp.max(s_pre, axis=-1), jnp.max(s_own, axis=-1))
    w_pre = jnp.exp(s_pre - row_top[..., None])
    w_own = jnp.exp(s_own - row_top[..., None])
    total = jnp.sum(w_pre, axis=-1) + jnp.sum(w_own, axis=-1)
    numer = jnp.einsum("kgct,tkd->kgcd", widen(w_pre.astype(jnp.bfloat16)), pre_vals, precision=highest)
    numer = numer + jnp.einsum("kgij,jkd->kgid", widen(w_own.astype(jnp.bfloat16)), own_vals, precision=highest)
    lse = row_top + jnp.log(total)
    result = jnp.transpose(numer / total[..., None], (2, 0, 1, 3)).reshape(COMP_LEN, Q_HEADS * HEAD_DIM)
    attended = jnp.where(live_rows[:, None], result, 0.0).astype(jnp.bfloat16)
    out_f = widen(attended).reshape(COMP_LEN, KV_HEADS, Q_PER_KV, HEAD_DIM)
    dsum = jnp.transpose(jnp.sum(out_f * grad_f, axis=-1), (1, 2, 0))
    row_mask = live_rows.astype(jnp.float32)[None, None, :, None]
    p_pre = jnp.exp(s_pre - lse[..., None]) * row_mask
    p_own = jnp.exp(s_own - lse[..., None]) * row_mask
    dp_pre = jnp.einsum("ckgd,tkd->kgct", grad_f, pre_vals, precision=highest)
    dp_own = jnp.einsum("ikgd,jkd->kgij", grad_f, own_vals, precision=highest)
    ds_pre = widen((p_pre * (dp_pre - dsum[..., None])).astype(jnp.bfloat16))
    ds_own = widen((p_own * (dp_own - dsum[..., None])).astype(jnp.bfloat16))
    pb_pre = widen(p_pre.astype(jnp.bfloat16))
    pb_own = widen(p_own.astype(jnp.bfloat16))
    grad_q = jnp.einsum("kgct,tkd->ckgd", ds_pre, pre_keys, precision=highest)
    grad_q = (grad_q + jnp.einsum("kgij,jkd->ikgd", ds_own, own_keys, precision=highest)) * inv_root
    dk_pre = jnp.einsum("kgct,ckgd->tkd", ds_pre, query_f, precision=highest) * inv_root
    dv_pre = jnp.einsum("kgct,ckgd->tkd", pb_pre, grad_f, precision=highest)
    dk_own = jnp.einsum("kgij,ikgd->jkd", ds_own, query_f, precision=highest) * inv_root
    dv_own = jnp.einsum("kgij,ikgd->jkd", pb_own, grad_f, precision=highest)
    kv_width = KV_HEADS * HEAD_DIM
    return (attended,
            grad_q.reshape(COMP_LEN, Q_HEADS * HEAD_DIM).astype(jnp.bfloat16),
            dk_own.reshape(COMP_LEN, kv_width).astype(jnp.bfloat16),
            dv_own.reshape(COMP_LEN, kv_width).astype(jnp.bfloat16),
            dk_pre.reshape(PREFIX, kv_width),
            dv_pre.reshape(PREFIX, kv_width))


def reference(prefix_k, prefix_v, queries, comp_k, comp_v, out_grad, lengths, owner_map):
    groups = jnp.arange(PROMPTS, dtype=jnp.int32)
    holder = jnp.sum(jnp.where(owner_map[None, :] == groups[:, None], groups[None, :], 0), axis=1).astype(jnp.int32)
    kv_width = KV_HEADS * HEAD_DIM
    init = (jnp.zeros((PROMPTS, PREFIX, kv_width), jnp.float32), jnp.zeros((PROMPTS, PREFIX, kv_width), jnp.float32))

    def block_step(carry, comp_no):
        sum_k, sum_v = carry
        prompt_no = holder[comp_no // PER_PROMPT].astype(jnp.int32)
        key_pre = lax.dynamic_index_in_dim(prefix_k, prompt_no, 0, keepdims=False)
        value_pre = lax.dynamic_index_in_dim(prefix_v, prompt_no, 0, keepdims=False)
        outputs = attend_one(queries[comp_no], key_pre, value_pre, comp_k[comp_no], comp_v[comp_no],
                             out_grad[comp_no], lengths[comp_no])
        sum_k = sum_k.at[prompt_no].add(outputs[4])
        sum_v = sum_v.at[prompt_no].add(outputs[5])
        return (sum_k, sum_v), outputs[:4]

    (sum_k, sum_v), stacked = lax.scan(block_step, init, jnp.arange(COMPLETIONS, dtype=jnp.int32))
    return stacked[0], stacked[1], stacked[2], stacked[3], sum_k, sum_v
```

```python
import functools

import jax
import jax.numpy as jnp
from jax import lax
from jax.experimental import pallas as pl
from jax.experimental.pallas import tpu as pltpu
from jax.sharding import PartitionSpec as P

KV_HEADS = 4
HEAD_DIM = 128
COMP_LEN = 256
Q_PER_KV = 5
SHARD = 128
SIDE = 4
PREFIX = SIDE * SIDE * SHARD
TOTAL = PREFIX + COMP_LEN

INV_ROOT = HEAD_DIM**-0.5
EXP2_SCALE = INV_ROOT * 1.4426950408889634
VERY_LOW = -1e30

SHIFTS = (0, 1, 3, 2)

GATHER_GROUPS = ((0,), (1, 2, 3))
CALL_GROUPS = ((0,), (1,), (2,), (3,))
REDUCE_GROUPS = ((0, 1), (2, 3))

NN = (((1,), (0,)), ((), ()))
NT = (((1,), (1,)), ((), ()))


def mxu(left, right, dims):
    return lax.dot_general(left, right, dims, preferred_element_type=jnp.float32)


def attend_kernel(tile, n_alias, at_ref, q_ref, g_ref, ck_ref, cv_ref, *rest):
    kept, crossed = rest[0:4], rest[4]
    att_ref, dq_ref, dck_ref, dcv_ref, keep_ref, send_ref = rest[5 + n_alias : 11 + n_alias]
    keys, vals, acc_k, acc_v = rest[11 + n_alias :]
    core = at_ref[1]
    member = pl.program_id(1)
    own = pl.ds(PREFIX, COMP_LEN)

    def fill(mine, theirs):
        for a in range(SIDE):
            for b in range(SIDE):
                mine[pl.ds((a * SIDE + b) * SHARD, SHARD), :] = kept[a][0, b]
                theirs[pl.ds((b * SIDE + a) * SHARD, SHARD), :] = crossed[a, b]

    @pl.when((member == 0) & (core == 0))
    def _():
        fill(keys, vals)

    @pl.when((member == 0) & (core == 1))
    def _():
        fill(vals, keys)

    @pl.when(member == 0)
    def _():
        keys[own, :] = ck_ref[...]
        vals[own, :] = cv_ref[...]
        acc_k[...] = jnp.zeros_like(acc_k)
        acc_v[...] = jnp.zeros_like(acc_v)

    query = q_ref[...]
    grad = g_ref[...]
    spans = [pl.ds(t, tile) for t in range(0, PREFIX, tile)] + [own]
    row_no = lax.broadcasted_iota(jnp.int32, (COMP_LEN, COMP_LEN), 0)
    col_no = lax.broadcasted_iota(jnp.int32, (COMP_LEN, COMP_LEN), 1)
    scores = [mxu(query, keys[span, :], NT) for span in spans]
    scores[-1] = jnp.where(col_no <= row_no, scores[-1], VERY_LOW)
    top = functools.reduce(jnp.maximum, [jnp.max(s, axis=1, keepdims=True) for s in scores])
    top = top * EXP2_SCALE
    weights = [jnp.exp2(s * EXP2_SCALE - top) for s in scores]
    total = sum(jnp.sum(w, axis=1, keepdims=True) for w in weights)
    weights_bf = [w.astype(jnp.bfloat16) for w in weights]
    numer = sum(mxu(w, vals[span, :], NN) for w, span in zip(weights_bf, spans))
    live = lax.broadcasted_iota(jnp.int32, (COMP_LEN, 1), 0) < at_ref[0]
    inv_total = jnp.where(live, 1.0 / total, 0.0)
    attended = (numer * inv_total).astype(jnp.bfloat16)
    att_ref[...] = attended
    grad_wide = grad.astype(jnp.float32)
    dsum = jnp.sum(attended.astype(jnp.float32) * grad_wide, axis=1, keepdims=True)
    grad_t = (grad_wide * inv_total).astype(jnp.bfloat16).T
    query_t = (query.astype(jnp.float32) * (inv_total * INV_ROOT)).astype(jnp.bfloat16).T
    dq = 0.0
    for span, w, w_bf in zip(spans, weights, weights_bf):
        dweight = mxu(grad, vals[span, :], NT)
        dscore = (w * (dweight - dsum)).astype(jnp.bfloat16)
        dq = dq + mxu(dscore, keys[span, :], NN)
        acc_k[:, span] += mxu(query_t, dscore, NN)
        acc_v[:, span] += mxu(grad_t, w_bf, NN)
    dq_ref[...] = (dq * (inv_total * INV_ROOT)).astype(jnp.bfloat16)

    def empty(mine, theirs):
        for a in range(SIDE):
            for b in range(SIDE):
                cols = pl.ds((a * SIDE + b) * SHARD, SHARD)
                keep_ref[a, b] = mine[:, cols].T.astype(jnp.bfloat16)
                cols = pl.ds((b * SIDE + a) * SHARD, SHARD)
                send_ref[a, b] = theirs[:, cols].T.astype(jnp.bfloat16)

    @pl.when((member == Q_PER_KV - 1) & (core == 0))
    def _():
        empty(acc_k, acc_v)

    @pl.when((member == Q_PER_KV - 1) & (core == 1))
    def _():
        empty(acc_v, acc_k)

    @pl.when(member == Q_PER_KV - 1)
    def _():
        dck_ref[...] = acc_k[:, own].T.astype(jnp.bfloat16)
        dcv_ref[...] = acc_v[:, own].T.astype(jnp.bfloat16)


def attend(heads, at, rows_in, kept, crossed, in_at, out_at, out_heads, held, grads):
    first = heads[0]
    per_head = pl.BlockSpec(
        (COMP_LEN, HEAD_DIM), lambda h, j, _: (0, (h + first) * Q_PER_KV + j)
    )
    per_kv = pl.BlockSpec((COMP_LEN, HEAD_DIM), lambda h, j, _: (0, h + first))
    kept_in = pl.BlockSpec((1, SIDE, SHARD, HEAD_DIM), lambda h, j, _: (0, 0, 0, h + in_at))
    square = (SIDE, SIDE, SHARD, HEAD_DIM)
    crossed_in = pl.BlockSpec(square, lambda h, j, _: (0, 0, 0, h + in_at))
    square_out = pl.BlockSpec(square, lambda h, j, _: (0, 0, 0, h + out_at))
    wide = jax.ShapeDtypeStruct((COMP_LEN, KV_HEADS * Q_PER_KV * HEAD_DIM), jnp.bfloat16)
    narrow = jax.ShapeDtypeStruct((COMP_LEN, KV_HEADS * HEAD_DIM), jnp.bfloat16)
    part = jax.ShapeDtypeStruct((SIDE, SIDE, SHARD, out_heads * HEAD_DIM), jnp.bfloat16)
    extra, aliases = [], {}
    base = 1 + 4 + 5
    for out_no, item in enumerate((held or [None] * 4) + (grads or [None] * 2)):
        if item is not None:
            aliases[base + len(extra)] = out_no
            extra.append(item)
    return pl.pallas_call(
        functools.partial(attend_kernel, 1024, len(extra)),
        grid_spec=pltpu.PrefetchScalarGridSpec(
            num_scalar_prefetch=1,
            grid=(len(heads), Q_PER_KV),
            in_specs=[per_head, per_head, per_kv, per_kv]
            + [kept_in] * 4
            + [crossed_in]
            + [pl.BlockSpec(memory_space=pl.ANY)] * len(extra),
            out_specs=[per_head, per_head, per_kv, per_kv] + [square_out] * 2,
            scratch_shapes=[pltpu.VMEM((TOTAL, HEAD_DIM), jnp.bfloat16)] * 2
            + [pltpu.VMEM((HEAD_DIM, TOTAL), jnp.float32)] * 2,
        ),
        out_shape=[wide, wide, narrow, narrow] + [part] * 2,
        input_output_aliases=aliases,
        compiler_params=pltpu.CompilerParams(vmem_limit_bytes=60 * 2**20),
        cost_estimate=pl.CostEstimate(
            flops=len(heads) * 6 * 2 * Q_PER_KV * COMP_LEN * TOTAL * HEAD_DIM,
            bytes_accessed=len(heads) * 5 * 2**20,
            transcendentals=len(heads) * Q_PER_KV * COMP_LEN * TOTAL,
        ),
    )(at, *rows_in, *kept, crossed, *extra)


def move_plane(item, shift, first):
    pairs = []
    for p in range(8):
        along_x = (p % 2 == 0) == first
        for x in range(SIDE):
            for y in range(SIDE):
                to_x = (x + shift) % SIDE if along_x else x
                to_y = y if along_x else (y + shift) % SIDE
                pairs.append(((p * SIDE + x) * SIDE + y, (p * SIDE + to_x) * SIDE + to_y))
    return lax.ppermute(item, ("prompt", "learner"), pairs)


def move_z(item, shift):
    pairs = [(z * 2 + c, ((z + shift) % 4) * 2 + c) for z in range(4) for c in range(2)]
    return lax.ppermute(item, "prompt", pairs)


def swap_cores(item):
    return lax.ppermute(item, "prompt", [(p, p ^ 1) for p in range(8)])


def spread(item, first):
    return [move_plane(item, s, first) if s else item for s in SHIFTS]


class Place:
    def __init__(self, source_of):
        here = lax.axis_index("prompt")
        self.z, self.core = here // 2, here % 2
        self.mine = lax.dynamic_index_in_dim(source_of, here, 0, keepdims=False)
        self.other = lax.dynamic_index_in_dim(source_of, here ^ 1, 0, keepdims=False)

    def of(self, column, who):
        return lax.select_n((self.z - who // 2) % 4, *column)


def tie(*trees):
    return lax.optimization_barrier(trees)


def bring_column(item):
    return [item] + [move_z(item, s) for s in (1, 2, 3)]


def choose(column, place):
    mine, other = place.of(column, place.mine), place.of(column, place.other)
    on_first = place.core == 0
    send = jnp.stack([jnp.where(on_first, p[1], p[0]) for p in (other, mine)])
    keep = jnp.stack([jnp.where(on_first, p[0], p[1]) for p in (mine, other)])
    return keep, send


def join(keep, got, place):
    same_core = jnp.stack([place.mine, place.other]) % 2 == place.core
    return jnp.where(same_core[:, None, None], keep, got)


def bring_row(pair):
    return jnp.stack(spread(pair, True), axis=1)


def cross(kept):
    return swap_cores(jnp.stack([part[1] for part in kept]))


def return_row(keep, got):
    return [jnp.stack([keep[a], got[a]]) for a in range(SIDE)]


def move_back(items, first):
    return [move_plane(item, -s, first) if s else item for item, s in zip(items, SHIFTS)]


def add_up(items):
    return sum(item.astype(jnp.float32) for item in items).astype(jnp.bfloat16)


def give_back(row, place):
    pair = add_up(move_back([row[:, b] for b in range(SIDE)], True))
    column = [pair] + [move_z(pair, s) for s in (1, 2, 3)]

    def pick(who):
        both = place.of(column, who)
        return jnp.where(who % 2 == place.core, both[0], both[1])

    kept = pick(place.mine)
    crossed = swap_cores(pick(place.other))
    on_first = place.core == 0
    dk = jnp.where(on_first, kept, crossed)
    dv = jnp.where(on_first, crossed, kept)
    return dk.astype(jnp.float32), dv.astype(jnp.float32)


def body(prefix_k, prefix_v, queries, comp_k, comp_v, out_grad, lengths, owner_map):
    n_learn = lax.axis_size("learner")
    here = lax.axis_index("prompt")
    me = here * n_learn + lax.axis_index("learner")
    groups = jnp.arange(owner_map.shape[0], dtype=jnp.int32)
    holder = jnp.sum(jnp.where(owner_map[None, :] == groups[:, None], groups[None, :], 0), axis=1)
    my_len = lax.dynamic_index_in_dim(lengths, me, 0, keepdims=False)
    at = jnp.stack([my_len, here % 2])
    rows_in = [queries[0], out_grad[0], comp_k[0], comp_v[0]]

    place = Place(holder)
    first, rest = [
        jnp.stack([t[0, :, g[0] * HEAD_DIM : (g[-1] + 1) * HEAD_DIM] for t in (prefix_k, prefix_v)])
        for g in GATHER_GROUPS
    ]
    column = bring_column(first)
    keep, send = choose(column, place)
    send, rest = tie(send, rest)
    got = swap_cores(send)
    rest_column = bring_column(rest)
    row = bring_row(join(keep, got, place))
    rest_keep, rest_send = choose(rest_column, place)
    rest_send, row = tie(rest_send, row)
    kept = spread(row, False)
    rest_got = swap_cores(rest_send)
    rest_row = bring_row(join(rest_keep, rest_got, place))
    crossed = cross(kept)
    crossed, kept, rest_row = tie(crossed, kept, rest_row)
    rest_kept = spread(rest_row, False)

    width = len(REDUCE_GROUPS[0])

    def call(head, source, in_at, held, grads):
        outs = attend((head,), at, rows_in, *source, in_at, head % width, width, held, grads)
        return list(outs[:4]), list(outs[4:])

    held, _sums = call(0, (kept, crossed), 0, None, None)
    _sums, rest_kept = tie(_sums, rest_kept)
    rest_source = (rest_kept, cross(rest_kept))
    held, (keep, send) = call(1, rest_source, 0, held, _sums)
    got = swap_cores(send)
    held, _sums = call(2, rest_source, 1, held, None)
    held, got = tie(held, got)
    back = move_back(return_row(keep, got), False)
    held, (rest_keep, rest_send) = call(3, rest_source, 2, held, _sums)
    rest_send, back = tie(rest_send, back)
    rest_got = swap_cores(rest_send)
    place = Place(owner_map)
    rest_back = move_back(return_row(rest_keep, rest_got), False)
    grads = [give_back(add_up(b), place) for b in (back, rest_back)]
    attended, grad_queries, grad_comp_k, grad_comp_v = held
    return (
        attended[None],
        grad_queries[None],
        grad_comp_k[None],
        grad_comp_v[None],
        jnp.concatenate([dk for dk, _ in grads], axis=1)[None],
        jnp.concatenate([dv for _, dv in grads], axis=1)[None],
    )


def solution(mesh):
    by_prompt = P("prompt", "learner", None)
    by_completion = P(("prompt", "learner"), None, None)
    return jax.shard_map(
        body,
        mesh=mesh,
        in_specs=(by_prompt,) * 2 + (by_completion,) * 4 + (P(), P()),
        out_specs=(by_completion,) * 4 + (by_prompt,) * 2,
        check_vma=False,
    )
```

```python
import functools

import jax
import jax.numpy as jnp
from jax import lax
from jax.experimental import pallas as pl
from jax.experimental.pallas import tpu as pltpu
from jax.sharding import PartitionSpec as P

KV_HEADS = 4
HEAD_DIM = 128
COMP_LEN = 256
Q_PER_KV = 5
SHARD = 128
SIDE = 4
PREFIX = SIDE * SIDE * SHARD
TOTAL = PREFIX + COMP_LEN

INV_ROOT = HEAD_DIM**-0.5
EXP2_SCALE = INV_ROOT * 1.4426950408889634
VERY_LOW = -1e30

SHIFTS = (0, 2, 1, 3)

GATHER_GROUPS = ((0,), (1, 2, 3))

NN = (((1,), (0,)), ((), ()))
NT = (((1,), (1,)), ((), ()))


def mxu(left, right, dims):
    return lax.dot_general(left, right, dims, preferred_element_type=jnp.float32)


def attend_kernel(tile, n_alias, at_ref, q_ref, g_ref, ck_ref, cv_ref, *rest):
    kept, crossed = rest[0:4], rest[4]
    att_ref, dq_ref, dck_ref, dcv_ref, keep_ref, send_ref = rest[5 + n_alias : 11 + n_alias]
    keys, vals, acc_k, acc_v = rest[11 + n_alias :]
    core = at_ref[1]
    own = pl.ds(PREFIX, COMP_LEN)
    spans = [pl.ds(t, tile) for t in range(0, PREFIX, tile)] + [own]

    def fill(mine, theirs):
        for a in range(SIDE):
            for b in range(SIDE):
                mine[pl.ds((a * SIDE + b) * SHARD, SHARD), :] = kept[a][0, b]
                theirs[pl.ds((b * SIDE + a) * SHARD, SHARD), :] = crossed[a, b]

    @pl.when(core == 0)
    def _():
        fill(keys, vals)

    @pl.when(core == 1)
    def _():
        fill(vals, keys)

    keys[own, :] = ck_ref[...]
    vals[own, :] = cv_ref[...]
    row_no = lax.broadcasted_iota(jnp.int32, (COMP_LEN, COMP_LEN), 0)
    col_no = lax.broadcasted_iota(jnp.int32, (COMP_LEN, COMP_LEN), 1)
    visible = col_no <= row_no
    live = lax.broadcasted_iota(jnp.int32, (COMP_LEN, 1), 0) < at_ref[0]

    def score(member):
        query = q_ref[:, pl.ds(member * HEAD_DIM, HEAD_DIM)]
        scores = [mxu(query, keys[span, :], NT) for span in spans]
        scores[-1] = jnp.where(visible, scores[-1], VERY_LOW)
        top = functools.reduce(jnp.maximum, [jnp.max(s, axis=1, keepdims=True) for s in scores])
        return query, scores, top * EXP2_SCALE

    def forward(member, scores, top):
        grad = g_ref[:, pl.ds(member * HEAD_DIM, HEAD_DIM)]
        dweights = [mxu(grad, vals[span, :], NT) for span in spans]
        weights = [jnp.exp2(s * EXP2_SCALE - top) for s in scores]
        total = sum(jnp.sum(w, axis=1, keepdims=True) for w in weights)
        weights_bf = [w.astype(jnp.bfloat16) for w in weights]
        numer = sum(mxu(w, vals[span, :], NN) for w, span in zip(weights_bf, spans))
        return grad, dweights, weights, weights_bf, total, numer

    def backward(member, query, grad, dweights, weights, weights_bf, total, numer):
        cols = pl.ds(member * HEAD_DIM, HEAD_DIM)
        inv_total = jnp.where(live, 1.0 / total, 0.0)
        attended = (numer * inv_total).astype(jnp.bfloat16)
        att_ref[:, cols] = attended
        grad_wide = grad.astype(jnp.float32)
        dsum = jnp.sum(attended.astype(jnp.float32) * grad_wide, axis=1, keepdims=True)
        grad_t = (grad_wide * inv_total).astype(jnp.bfloat16).T
        query_t = (query.astype(jnp.float32) * (inv_total * INV_ROOT)).astype(jnp.bfloat16).T
        dq = 0.0
        for span, dweight, w, w_bf in zip(spans, dweights, weights, weights_bf):
            dscore = (w * (dweight - dsum)).astype(jnp.bfloat16)
            dq = dq + mxu(dscore, keys[span, :], NN)
            dk, dv = mxu(query_t, dscore, NN), mxu(grad_t, w_bf, NN)
            if member:
                acc_k[:, span] += dk
                acc_v[:, span] += dv
            else:
                acc_k[:, span] = dk
                acc_v[:, span] = dv
        dq_ref[:, cols] = (dq * (inv_total * INV_ROOT)).astype(jnp.bfloat16)

    ahead = score(0)
    for member in range(Q_PER_KV):
        query, scores, top = ahead
        done = forward(member, scores, top)
        if member + 1 < Q_PER_KV:
            ahead = score(member + 1)
        backward(member, query, *done)

    def empty(mine, theirs):
        for a in range(SIDE):
            for b in range(SIDE):
                cols = pl.ds((a * SIDE + b) * SHARD, SHARD)
                keep_ref[a, b] = mine[:, cols].T.astype(jnp.bfloat16)
                cols = pl.ds((b * SIDE + a) * SHARD, SHARD)
                send_ref[a, b] = theirs[:, cols].T.astype(jnp.bfloat16)

    @pl.when(core == 0)
    def _():
        empty(acc_k, acc_v)

    @pl.when(core == 1)
    def _():
        empty(acc_v, acc_k)

    dck_ref[...] = acc_k[:, own].T.astype(jnp.bfloat16)
    dcv_ref[...] = acc_v[:, own].T.astype(jnp.bfloat16)


def attend(heads, at, rows_in, kept, crossed, in_at, out_at, out_heads, held, grads):
    first = heads[0]
    per_head = pl.BlockSpec(
        (COMP_LEN, Q_PER_KV * HEAD_DIM), lambda h, _: (0, h + first)
    )
    per_kv = pl.BlockSpec((COMP_LEN, HEAD_DIM), lambda h, _: (0, h + first))
    kept_in = pl.BlockSpec((1, SIDE, SHARD, HEAD_DIM), lambda h, _: (0, 0, 0, h + in_at))
    square = (SIDE, SIDE, SHARD, HEAD_DIM)
    crossed_in = pl.BlockSpec(square, lambda h, _: (0, 0, 0, h + in_at))
    square_out = pl.BlockSpec(square, lambda h, _: (0, 0, 0, h + out_at))
    wide = jax.ShapeDtypeStruct((COMP_LEN, KV_HEADS * Q_PER_KV * HEAD_DIM), jnp.bfloat16)
    narrow = jax.ShapeDtypeStruct((COMP_LEN, KV_HEADS * HEAD_DIM), jnp.bfloat16)
    part = jax.ShapeDtypeStruct((SIDE, SIDE, SHARD, out_heads * HEAD_DIM), jnp.bfloat16)
    extra, aliases = [], {}
    base = 1 + 4 + 5
    for out_no, item in enumerate((held or [None] * 4) + (grads or [None] * 2)):
        if item is not None:
            aliases[base + len(extra)] = out_no
            extra.append(item)
    return pl.pallas_call(
        functools.partial(attend_kernel, 512, len(extra)),
        grid_spec=pltpu.PrefetchScalarGridSpec(
            num_scalar_prefetch=1,
            grid=(len(heads),),
            in_specs=[per_head, per_head, per_kv, per_kv]
            + [kept_in] * 4
            + [crossed_in]
            + [pl.BlockSpec(memory_space=pl.ANY)] * len(extra),
            out_specs=[per_head, per_head, per_kv, per_kv] + [square_out] * 2,
            scratch_shapes=[pltpu.VMEM((TOTAL, HEAD_DIM), jnp.bfloat16)] * 2
            + [pltpu.VMEM((HEAD_DIM, TOTAL), jnp.float32)] * 2,
        ),
        out_shape=[wide, wide, narrow, narrow] + [part] * 2,
        input_output_aliases=aliases,
        compiler_params=pltpu.CompilerParams(vmem_limit_bytes=60 * 2**20),
        cost_estimate=pl.CostEstimate(
            flops=len(heads) * 6 * 2 * Q_PER_KV * COMP_LEN * TOTAL * HEAD_DIM,
            bytes_accessed=len(heads) * 5 * 2**20,
            transcendentals=len(heads) * Q_PER_KV * COMP_LEN * TOTAL,
        ),
    )(at, *rows_in, *kept, crossed, *extra)


def move_plane(item, shift, first):
    pairs = []
    for p in range(8):
        along_x = (p % 2 == 0) == first
        for x in range(SIDE):
            for y in range(SIDE):
                to_x = (x + shift) % SIDE if along_x else x
                to_y = y if along_x else (y + shift) % SIDE
                pairs.append(((p * SIDE + x) * SIDE + y, (p * SIDE + to_x) * SIDE + to_y))
    return lax.ppermute(item, ("prompt", "learner"), pairs)


def move_z(item, shift):
    pairs = [(z * 2 + c, ((z + shift) % 4) * 2 + c) for z in range(4) for c in range(2)]
    return lax.ppermute(item, "prompt", pairs)


def swap_cores(item):
    return lax.ppermute(item, "prompt", [(p, p ^ 1) for p in range(8)])


def spread(item, first):
    return [move_plane(item, s, first) if s else item for s in SHIFTS]


class Place:
    def __init__(self, source_of):
        here = lax.axis_index("prompt")
        spot = jnp.arange(source_of.shape[0], dtype=jnp.int32)
        mine = jnp.sum(jnp.where(spot == here, source_of, 0))
        other = jnp.sum(jnp.where(spot == (here ^ 1), source_of, 0))
        self.first = (here & 1) == 0
        self.steps = [((here >> 1) - (who >> 1)) & 3 for who in (mine, other)]
        self.same = [((who ^ here) & 1) == 0 for who in (mine, other)]

    def of(self, column, which):
        step = self.steps[which]
        low = jnp.where((step & 1) == 0, column[0], column[1])
        high = jnp.where((step & 1) == 0, column[2], column[3])
        return jnp.where(step < 2, low, high)


def tie(*trees):
    return lax.optimization_barrier(trees)


def bring_column(item):
    far, near, back = [move_z(item, s) for s in (2, 1, 3)]
    return [item, near, far, back]


def choose(column, place):
    mine, other = place.of(column, 0), place.of(column, 1)
    send = jnp.stack([jnp.where(place.first, p[1], p[0]) for p in (other, mine)])
    keep = jnp.stack([jnp.where(place.first, p[0], p[1]) for p in (mine, other)])
    return keep, send


def join(keep, got, place):
    return jnp.stack([jnp.where(place.same[i], keep[i], got[i]) for i in range(2)])


def bring_row(pair):
    return jnp.stack(spread(pair, True), axis=1)


def cross(kept):
    return swap_cores(jnp.stack([part[1] for part in kept]))


def return_row(keep, got):
    return [jnp.stack([keep[a], got[a]]) for a in range(SIDE)]


def move_back(items, first):
    return [move_plane(item, -s, first) if s else item for item, s in zip(items, SHIFTS)]


def add_up(items):
    return sum(item.astype(jnp.float32) for item in items).astype(jnp.bfloat16)


def give_back(row, place):
    pair = add_up(move_back([row[:, b] for b in range(SIDE)], True))
    column = bring_column(pair)

    def pick(which, same):
        both = place.of(column, which)
        return jnp.where(same, both[0], both[1])

    kept = pick(0, place.same[0])
    crossed = swap_cores(pick(1, place.same[1]))
    dk = jnp.where(place.first, kept, crossed)
    dv = jnp.where(place.first, crossed, kept)
    return dk.astype(jnp.float32)[None], dv.astype(jnp.float32)[None]


def body(prefix_k, prefix_v, queries, comp_k, comp_v, out_grad, lengths, owner_map):
    n_learn = lax.axis_size("learner")
    here = lax.axis_index("prompt")
    me = here * n_learn + lax.axis_index("learner")
    groups = jnp.arange(owner_map.shape[0], dtype=jnp.int32)
    holder = jnp.sum(jnp.where(owner_map[None, :] == groups[:, None], groups[None, :], 0), axis=1)
    my_len = lax.dynamic_index_in_dim(lengths, me, 0, keepdims=False)
    at = jnp.stack([my_len, here % 2])
    rows_in = [queries[0], out_grad[0], comp_k[0], comp_v[0]]

    place = Place(holder)
    keep, send = choose(bring_column(jnp.stack([prefix_k[0], prefix_v[0]])), place)
    row = bring_row(join(keep, swap_cores(send), place))
    rows = [row[..., g[0] * HEAD_DIM : (g[-1] + 1) * HEAD_DIM] for g in GATHER_GROUPS]
    kept = spread(rows[0], False)
    kept, rest_row = tie(kept, rows[1])
    crossed = cross(kept)
    rest_kept = spread(rest_row, False)

    def call(group, kept, crossed, held):
        outs = attend(group, at, rows_in, kept, crossed, 0, 0, len(group), held, None)
        return list(outs[:4]), list(outs[4:])

    held, (keep, send) = call(GATHER_GROUPS[0], kept, crossed, None)
    send, rest_kept = tie(send, rest_kept)
    got = swap_cores(send)
    rest_crossed = cross(rest_kept)
    rest_crossed, got = tie(rest_crossed, got)
    back = move_back(return_row(keep, got), False)
    held, (rest_keep, rest_send) = call(GATHER_GROUPS[1], rest_kept, rest_crossed, held)
    rest_send, back = tie(rest_send, back)
    rest_back = move_back(return_row(rest_keep, swap_cores(rest_send)), False)
    row = jnp.concatenate([add_up(back), add_up(rest_back)], axis=-1)
    grad_prefix_k, grad_prefix_v = give_back(row, Place(owner_map))
    attended, grad_queries, grad_comp_k, grad_comp_v = held
    return (
        attended[None],
        grad_queries[None],
        grad_comp_k[None],
        grad_comp_v[None],
        grad_prefix_k,
        grad_prefix_v,
    )


def solution(mesh):
    by_prompt = P("prompt", "learner", None)
    by_completion = P(("prompt", "learner"), None, None)
    return jax.shard_map(
        body,
        mesh=mesh,
        in_specs=(by_prompt,) * 2 + (by_completion,) * 4 + (P(), P()),
        out_specs=(by_completion,) * 4 + (by_prompt,) * 2,
        check_vma=False,
    )
```

```python
import functools

import jax
import jax.numpy as jnp
from jax import lax
from jax.experimental import pallas as pl
from jax.experimental.pallas import tpu as pltpu
from jax.sharding import PartitionSpec as P

KV_HEADS = 4
HEAD_DIM = 128
COMP_LEN = 256
Q_PER_KV = 5
SHARD = 128
SIDE = 4
PREFIX = SIDE * SIDE * SHARD
TOTAL = PREFIX + COMP_LEN

INV_ROOT = HEAD_DIM**-0.5
EXP2_SCALE = INV_ROOT * 1.4426950408889634
VERY_LOW = -1e30

SHIFTS = (0, 2, 1, 3)

GATHER_GROUPS = ((0, 1), (2, 3))

NN = (((1,), (0,)), ((), ()))
NT = (((1,), (1,)), ((), ()))


def mxu(left, right, dims):
    return lax.dot_general(left, right, dims, preferred_element_type=jnp.float32)


def attend_kernel(tile, n_alias, len_ref, q_ref, g_ref, ck_ref, cv_ref, *rest):
    kept, crossed = rest[0:4], rest[4]
    att_ref, dq_ref, dck_ref, dcv_ref, keep_ref, send_ref = rest[5 + n_alias : 11 + n_alias]
    keys, vals, acc_k, acc_v = rest[11 + n_alias :]
    here = lax.axis_index("prompt")
    core = here & 1
    length = len_ref[here * lax.axis_size("learner") + lax.axis_index("learner")]
    own = pl.ds(PREFIX, COMP_LEN)
    spans = [pl.ds(t, tile) for t in range(0, PREFIX, tile)] + [own]

    def fill(mine, theirs):
        for a in range(SIDE):
            for b in range(SIDE):
                mine[pl.ds((a * SIDE + b) * SHARD, SHARD), :] = kept[a][0, b]
                theirs[pl.ds((b * SIDE + a) * SHARD, SHARD), :] = crossed[a, b]

    @pl.when(core == 0)
    def _():
        fill(keys, vals)

    @pl.when(core == 1)
    def _():
        fill(vals, keys)

    keys[own, :] = ck_ref[...]
    vals[own, :] = cv_ref[...]
    row_no = lax.broadcasted_iota(jnp.int32, (COMP_LEN, COMP_LEN), 0)
    col_no = lax.broadcasted_iota(jnp.int32, (COMP_LEN, COMP_LEN), 1)
    visible = col_no <= row_no
    live = lax.broadcasted_iota(jnp.int32, (COMP_LEN, 1), 0) < length

    def forward(member):
        query = q_ref[:, pl.ds(member * HEAD_DIM, HEAD_DIM)]
        scores = [mxu(query, keys[span, :], NT) for span in spans]
        scores[-1] = jnp.where(visible, scores[-1], VERY_LOW)
        top = functools.reduce(jnp.maximum, [jnp.max(s, axis=1, keepdims=True) for s in scores])
        top = top * EXP2_SCALE
        grad = g_ref[:, pl.ds(member * HEAD_DIM, HEAD_DIM)]
        dweights = [mxu(grad, vals[span, :], NT) for span in spans]
        weights = [jnp.exp2(s * EXP2_SCALE - top) for s in scores]
        total = sum(jnp.sum(w, axis=1, keepdims=True) for w in weights)
        weights_bf = [w.astype(jnp.bfloat16) for w in weights]
        numer = sum(mxu(w, vals[span, :], NN) for w, span in zip(weights_bf, spans))
        return query, grad, dweights, weights, weights_bf, total, numer

    def backward(member, query, grad, dweights, weights, weights_bf, total, numer):
        cols = pl.ds(member * HEAD_DIM, HEAD_DIM)
        inv_total = jnp.where(live, 1.0 / total, 0.0)
        attended = (numer * inv_total).astype(jnp.bfloat16)
        att_ref[:, cols] = attended
        grad_wide = grad.astype(jnp.float32)
        dsum = jnp.sum(attended.astype(jnp.float32) * grad_wide, axis=1, keepdims=True)
        grad_t = (grad_wide * inv_total).astype(jnp.bfloat16).T
        query_t = (query.astype(jnp.float32) * (inv_total * INV_ROOT)).astype(jnp.bfloat16).T
        dq = 0.0
        for span, dweight, w, w_bf in zip(spans, dweights, weights, weights_bf):
            dscore = (w * (dweight - dsum)).astype(jnp.bfloat16)
            dq = dq + mxu(dscore, keys[span, :], NN)
            dk, dv = mxu(query_t, dscore, NN), mxu(grad_t, w_bf, NN)
            if member:
                acc_k[:, span] += dk
                acc_v[:, span] += dv
            else:
                acc_k[:, span] = dk
                acc_v[:, span] = dv
        dq_ref[:, cols] = (dq * (inv_total * INV_ROOT)).astype(jnp.bfloat16)

    done = forward(0)
    for member in range(Q_PER_KV):
        ahead = forward(member + 1) if member + 1 < Q_PER_KV else None
        backward(member, *done)
        done = ahead

    def empty(mine, theirs):
        for a in range(SIDE):
            for b in range(SIDE):
                cols = pl.ds((a * SIDE + b) * SHARD, SHARD)
                keep_ref[a, b] = mine[:, cols].T.astype(jnp.bfloat16)
                cols = pl.ds((b * SIDE + a) * SHARD, SHARD)
                send_ref[a, b] = theirs[:, cols].T.astype(jnp.bfloat16)

    @pl.when(core == 0)
    def _():
        empty(acc_k, acc_v)

    @pl.when(core == 1)
    def _():
        empty(acc_v, acc_k)

    dck_ref[...] = acc_k[:, own].T.astype(jnp.bfloat16)
    dcv_ref[...] = acc_v[:, own].T.astype(jnp.bfloat16)


def attend(heads, lengths, rows_in, kept, crossed, in_at, out_at, out_heads, held, grads):
    first = heads[0]
    per_head = pl.BlockSpec(
        (COMP_LEN, Q_PER_KV * HEAD_DIM), lambda h, _: (0, h + first)
    )
    per_kv = pl.BlockSpec((COMP_LEN, HEAD_DIM), lambda h, _: (0, h + first))
    kept_in = pl.BlockSpec((1, SIDE, SHARD, HEAD_DIM), lambda h, _: (0, 0, 0, h + in_at))
    square = (SIDE, SIDE, SHARD, HEAD_DIM)
    crossed_in = pl.BlockSpec(square, lambda h, _: (0, 0, 0, h + in_at))
    square_out = pl.BlockSpec(square, lambda h, _: (0, 0, 0, h + out_at))
    wide = jax.ShapeDtypeStruct((COMP_LEN, KV_HEADS * Q_PER_KV * HEAD_DIM), jnp.bfloat16)
    narrow = jax.ShapeDtypeStruct((COMP_LEN, KV_HEADS * HEAD_DIM), jnp.bfloat16)
    part = jax.ShapeDtypeStruct((SIDE, SIDE, SHARD, out_heads * HEAD_DIM), jnp.bfloat16)
    extra, aliases = [], {}
    base = 1 + 4 + 5
    for out_no, item in enumerate((held or [None] * 4) + (grads or [None] * 2)):
        if item is not None:
            aliases[base + len(extra)] = out_no
            extra.append(item)
    return pl.pallas_call(
        functools.partial(attend_kernel, 512, len(extra)),
        grid_spec=pltpu.PrefetchScalarGridSpec(
            num_scalar_prefetch=1,
            grid=(len(heads),),
            in_specs=[per_head, per_head, per_kv, per_kv]
            + [kept_in] * 4
            + [crossed_in]
            + [pl.BlockSpec(memory_space=pl.ANY)] * len(extra),
            out_specs=[per_head, per_head, per_kv, per_kv] + [square_out] * 2,
            scratch_shapes=[pltpu.VMEM((TOTAL, HEAD_DIM), jnp.bfloat16)] * 2
            + [pltpu.VMEM((HEAD_DIM, TOTAL), jnp.float32)] * 2,
        ),
        out_shape=[wide, wide, narrow, narrow] + [part] * 2,
        input_output_aliases=aliases,
        compiler_params=pltpu.CompilerParams(vmem_limit_bytes=60 * 2**20),
        cost_estimate=pl.CostEstimate(
            flops=len(heads) * 6 * 2 * Q_PER_KV * COMP_LEN * TOTAL * HEAD_DIM,
            bytes_accessed=len(heads) * 5 * 2**20,
            transcendentals=len(heads) * Q_PER_KV * COMP_LEN * TOTAL,
        ),
    )(lengths, *rows_in, *kept, crossed, *extra)


def move_plane(item, shift, first):
    pairs = []
    for p in range(8):
        along_x = (p % 2 == 0) == first
        for x in range(SIDE):
            for y in range(SIDE):
                to_x = (x + shift) % SIDE if along_x else x
                to_y = y if along_x else (y + shift) % SIDE
                pairs.append(((p * SIDE + x) * SIDE + y, (p * SIDE + to_x) * SIDE + to_y))
    return lax.ppermute(item, ("prompt", "learner"), pairs)


def move_z(item, shift):
    pairs = [(z * 2 + c, ((z + shift) % 4) * 2 + c) for z in range(4) for c in range(2)]
    return lax.ppermute(item, "prompt", pairs)


def swap_cores(item):
    return lax.ppermute(item, "prompt", [(p, p ^ 1) for p in range(8)])


def spread(item, first):
    return [move_plane(item, s, first) if s else item for s in SHIFTS]


class Place:
    def __init__(self, source_of):
        here = lax.axis_index("prompt")
        spot = jnp.arange(source_of.shape[0], dtype=jnp.int32)
        mine = jnp.sum(jnp.where(spot == here, source_of, 0))
        other = jnp.sum(jnp.where(spot == (here ^ 1), source_of, 0))
        self.first = (here & 1) == 0
        self.steps = [((here >> 1) - (who >> 1)) & 3 for who in (mine, other)]
        self.same = [((who ^ here) & 1) == 0 for who in (mine, other)]

    def of(self, column, which):
        step = self.steps[which]
        low = jnp.where((step & 1) == 0, column[0], column[1])
        high = jnp.where((step & 1) == 0, column[2], column[3])
        return jnp.where(step < 2, low, high)


def tie(*trees):
    return lax.optimization_barrier(trees)


def bring_column(item):
    far, near, back = [move_z(item, s) for s in (2, 1, 3)]
    return [item, near, far, back]


def choose(column, place):
    mine, other = place.of(column, 0), place.of(column, 1)
    send = jnp.stack([jnp.where(place.first, p[1], p[0]) for p in (other, mine)])
    keep = jnp.stack([jnp.where(place.first, p[0], p[1]) for p in (mine, other)])
    return keep, send


def join(keep, got, place):
    return jnp.stack([jnp.where(place.same[i], keep[i], got[i]) for i in range(2)])


def bring_row(pair):
    return jnp.stack(spread(pair, True), axis=1)


def cross(kept):
    return swap_cores(jnp.stack([part[1] for part in kept]))


def return_row(keep, got):
    return [jnp.stack([keep[a], got[a]]) for a in range(SIDE)]


def move_back(items, first):
    return [move_plane(item, -s, first) if s else item for item, s in zip(items, SHIFTS)]


def add_up(items):
    return sum(item.astype(jnp.float32) for item in items).astype(jnp.bfloat16)


def give_back(row, place):
    pair = add_up(move_back([row[:, b] for b in range(SIDE)], True))
    column = bring_column(pair)

    def pick(which, same):
        both = place.of(column, which)
        return jnp.where(same, both[0], both[1])

    kept = pick(0, place.same[0])
    crossed = swap_cores(pick(1, place.same[1]))
    dk = jnp.where(place.first, kept, crossed)
    dv = jnp.where(place.first, crossed, kept)
    return dk.astype(jnp.float32)[None], dv.astype(jnp.float32)[None]


def body(prefix_k, prefix_v, queries, comp_k, comp_v, out_grad, lengths, owner_map):
    groups = jnp.arange(owner_map.shape[0], dtype=jnp.int32)
    holder = jnp.sum(jnp.where(owner_map[None, :] == groups[:, None], groups[None, :], 0), axis=1)
    rows_in = [queries[0], out_grad[0], comp_k[0], comp_v[0]]

    place = Place(holder)
    is_key = lax.broadcasted_iota(jnp.int32, (2, 1, 1), 0) == 0
    keep, send = choose(bring_column(jnp.where(is_key, prefix_k, prefix_v)), place)
    row = bring_row(join(keep, swap_cores(send), place))
    rows = [row[..., g[0] * HEAD_DIM : (g[-1] + 1) * HEAD_DIM] for g in GATHER_GROUPS]
    kept = spread(rows[0], False)
    kept, rest_row = tie(kept, rows[1])
    crossed = cross(kept)
    rest_kept = spread(rest_row, False)

    def call(group, kept, crossed, held):
        outs = attend(group, lengths, rows_in, kept, crossed, 0, 0, len(group), held, None)
        return list(outs[:4]), list(outs[4:])

    held, (keep, send) = call(GATHER_GROUPS[0], kept, crossed, None)
    send, rest_kept = tie(send, rest_kept)
    got = swap_cores(send)
    handed = jnp.stack([part[1] for part in rest_kept])
    handed, got = tie(handed, got)
    rest_crossed = swap_cores(handed)
    back = move_back(return_row(keep, got), False)
    held, (rest_keep, rest_send) = call(GATHER_GROUPS[1], rest_kept, rest_crossed, held)
    rest_send, back = tie(rest_send, back)
    rest_back = move_back(return_row(rest_keep, swap_cores(rest_send)), False)
    row = jnp.concatenate([add_up(back), add_up(rest_back)], axis=-1)
    grad_prefix_k, grad_prefix_v = give_back(row, Place(owner_map))
    attended, grad_queries, grad_comp_k, grad_comp_v = held
    return (
        attended[None],
        grad_queries[None],
        grad_comp_k[None],
        grad_comp_v[None],
        grad_prefix_k,
        grad_prefix_v,
    )


def solution(mesh):
    by_prompt = P("prompt", "learner", None)
    by_completion = P(("prompt", "learner"), None, None)
    return jax.shard_map(
        body,
        mesh=mesh,
        in_specs=(by_prompt,) * 2 + (by_completion,) * 4 + (P(), P()),
        out_specs=(by_completion,) * 4 + (by_prompt,) * 2,
        check_vma=False,
    )
```

```python
import functools

import jax
import jax.numpy as jnp
from jax import lax
from jax.experimental import pallas as pl
from jax.experimental.pallas import tpu as pltpu
from jax.sharding import PartitionSpec as P

KV_HEADS = 4
HEAD_DIM = 128
COMP_LEN = 256
Q_PER_KV = 5
SHARD = 128
SIDE = 4
PREFIX = SIDE * SIDE * SHARD
TOTAL = PREFIX + COMP_LEN

INV_ROOT = HEAD_DIM**-0.5
EXP2_SCALE = INV_ROOT * 1.4426950408889634
VERY_LOW = -1e30

SHIFTS = (0, 2, 1, 3)

GATHER_GROUPS = ((0, 1), (2, 3))

NN = (((1,), (0,)), ((), ()))
NT = (((1,), (1,)), ((), ()))


def mxu(left, right, dims):
    return lax.dot_general(left, right, dims, preferred_element_type=jnp.float32)


def attend_kernel(tile, n_alias, len_ref, q_ref, g_ref, ck_ref, cv_ref, *rest):
    kept, crossed = rest[0:4], rest[4]
    att_ref, dq_ref, dck_ref, dcv_ref, keep_ref, send_ref = rest[5 + n_alias : 11 + n_alias]
    keys, vals, acc_k, acc_v = rest[11 + n_alias :]
    here = lax.axis_index("prompt")
    core = here & 1
    length = len_ref[here * lax.axis_size("learner") + lax.axis_index("learner")]
    own = pl.ds(PREFIX, COMP_LEN)
    width = pl.ds(0, HEAD_DIM)
    spans = [pl.ds(t, tile) for t in range(0, PREFIX, tile)] + [own]

    def fill(mine, theirs):
        for a in range(SIDE):
            for b in range(SIDE):
                mine[pl.ds((a * SIDE + b) * SHARD, SHARD), width] = kept[a][0, b]
                theirs[pl.ds((b * SIDE + a) * SHARD, SHARD), width] = crossed[a, b]

    @pl.when(core == 0)
    def _():
        fill(keys, vals)

    @pl.when(core == 1)
    def _():
        fill(vals, keys)

    keys[own, :] = ck_ref[...]
    vals[own, width] = cv_ref[...]
    vals[:, pl.ds(HEAD_DIM, HEAD_DIM)] = jnp.ones((TOTAL, HEAD_DIM), jnp.bfloat16)
    row_no = lax.broadcasted_iota(jnp.int32, (COMP_LEN, COMP_LEN), 0)
    col_no = lax.broadcasted_iota(jnp.int32, (COMP_LEN, COMP_LEN), 1)
    visible = col_no <= row_no
    live = lax.broadcasted_iota(jnp.int32, (COMP_LEN, 1), 0) < length

    def forward(member):
        query = q_ref[:, pl.ds(member * HEAD_DIM, HEAD_DIM)]
        scores = [mxu(query, keys[span, :], NT) for span in spans]
        scores[-1] = jnp.where(visible, scores[-1], VERY_LOW)
        top = functools.reduce(jnp.maximum, [jnp.max(s, axis=1, keepdims=True) for s in scores])
        top = top * EXP2_SCALE
        grad = g_ref[:, pl.ds(member * HEAD_DIM, HEAD_DIM)]
        dweights = [mxu(grad, vals[span, width], NT) for span in spans]
        weights = [jnp.exp2(s * EXP2_SCALE - top) for s in scores]
        weights_bf = [w.astype(jnp.bfloat16) for w in weights]
        numer = sum(mxu(w, vals[span, :], NN) for w, span in zip(weights_bf, spans))
        numer, total = numer[:, :HEAD_DIM], numer[:, HEAD_DIM : HEAD_DIM + 1]
        return query, grad, dweights, weights, weights_bf, total, numer

    def backward(member, query, grad, dweights, weights, weights_bf, total, numer):
        cols = pl.ds(member * HEAD_DIM, HEAD_DIM)
        inv_total = jnp.where(live, 1.0 / total, 0.0)
        attended = (numer * inv_total).astype(jnp.bfloat16)
        att_ref[:, cols] = attended
        grad_wide = grad.astype(jnp.float32)
        dsum = jnp.sum(attended.astype(jnp.float32) * grad_wide, axis=1, keepdims=True)
        grad_t = (grad_wide * inv_total).astype(jnp.bfloat16).T
        query_t = (query.astype(jnp.float32) * (inv_total * INV_ROOT)).astype(jnp.bfloat16).T
        dq = 0.0
        for span, dweight, w, w_bf in zip(spans, dweights, weights, weights_bf):
            dscore = (w * (dweight - dsum)).astype(jnp.bfloat16)
            dq = dq + mxu(dscore, keys[span, :], NN)
            dk, dv = mxu(query_t, dscore, NN), mxu(grad_t, w_bf, NN)
            if member:
                acc_k[:, span] += dk
                acc_v[:, span] += dv
            else:
                acc_k[:, span] = dk
                acc_v[:, span] = dv
        dq_ref[:, cols] = (dq * (inv_total * INV_ROOT)).astype(jnp.bfloat16)

    done = forward(0)
    for member in range(Q_PER_KV):
        ahead = forward(member + 1) if member + 1 < Q_PER_KV else None
        backward(member, *done)
        done = ahead

    def empty(mine, theirs):
        for a in range(SIDE):
            for b in range(SIDE):
                cols = pl.ds((a * SIDE + b) * SHARD, SHARD)
                keep_ref[a, b] = mine[:, cols].T.astype(jnp.bfloat16)
                cols = pl.ds((b * SIDE + a) * SHARD, SHARD)
                send_ref[a, b] = theirs[:, cols].T.astype(jnp.bfloat16)

    @pl.when(core == 0)
    def _():
        empty(acc_k, acc_v)

    @pl.when(core == 1)
    def _():
        empty(acc_v, acc_k)

    dck_ref[...] = acc_k[:, own].T.astype(jnp.bfloat16)
    dcv_ref[...] = acc_v[:, own].T.astype(jnp.bfloat16)


def attend(heads, lengths, rows_in, kept, crossed, in_at, out_at, out_heads, held, grads):
    first = heads[0]
    per_head = pl.BlockSpec(
        (COMP_LEN, Q_PER_KV * HEAD_DIM), lambda h, _: (0, h + first)
    )
    per_kv = pl.BlockSpec((COMP_LEN, HEAD_DIM), lambda h, _: (0, h + first))
    kept_in = pl.BlockSpec((1, SIDE, SHARD, HEAD_DIM), lambda h, _: (0, 0, 0, h + in_at))
    square = (SIDE, SIDE, SHARD, HEAD_DIM)
    crossed_in = pl.BlockSpec(square, lambda h, _: (0, 0, 0, h + in_at))
    square_out = pl.BlockSpec(square, lambda h, _: (0, 0, 0, h + out_at))
    wide = jax.ShapeDtypeStruct((COMP_LEN, KV_HEADS * Q_PER_KV * HEAD_DIM), jnp.bfloat16)
    narrow = jax.ShapeDtypeStruct((COMP_LEN, KV_HEADS * HEAD_DIM), jnp.bfloat16)
    part = jax.ShapeDtypeStruct((SIDE, SIDE, SHARD, out_heads * HEAD_DIM), jnp.bfloat16)
    extra, aliases = [], {}
    base = 1 + 4 + 5
    for out_no, item in enumerate((held or [None] * 4) + (grads or [None] * 2)):
        if item is not None:
            aliases[base + len(extra)] = out_no
            extra.append(item)
    return pl.pallas_call(
        functools.partial(attend_kernel, 256, len(extra)),
        grid_spec=pltpu.PrefetchScalarGridSpec(
            num_scalar_prefetch=1,
            grid=(len(heads),),
            in_specs=[per_head, per_head, per_kv, per_kv]
            + [kept_in] * 4
            + [crossed_in]
            + [pl.BlockSpec(memory_space=pl.ANY)] * len(extra),
            out_specs=[per_head, per_head, per_kv, per_kv] + [square_out] * 2,
            scratch_shapes=[
                pltpu.VMEM((TOTAL, HEAD_DIM), jnp.bfloat16),
                pltpu.VMEM((TOTAL, 2 * HEAD_DIM), jnp.bfloat16),
            ]
            + [pltpu.VMEM((HEAD_DIM, TOTAL), jnp.float32)] * 2,
        ),
        out_shape=[wide, wide, narrow, narrow] + [part] * 2,
        input_output_aliases=aliases,
        compiler_params=pltpu.CompilerParams(vmem_limit_bytes=60 * 2**20),
        cost_estimate=pl.CostEstimate(
            flops=len(heads) * 6 * 2 * Q_PER_KV * COMP_LEN * TOTAL * HEAD_DIM,
            bytes_accessed=len(heads) * 5 * 2**20,
            transcendentals=len(heads) * Q_PER_KV * COMP_LEN * TOTAL,
        ),
    )(lengths, *rows_in, *kept, crossed, *extra)


def move_plane(item, shift, first):
    pairs = []
    for p in range(8):
        along_x = (p % 2 == 0) == first
        for x in range(SIDE):
            for y in range(SIDE):
                to_x = (x + shift) % SIDE if along_x else x
                to_y = y if along_x else (y + shift) % SIDE
                pairs.append(((p * SIDE + x) * SIDE + y, (p * SIDE + to_x) * SIDE + to_y))
    return lax.ppermute(item, ("prompt", "learner"), pairs)


def move_z(item, shift):
    pairs = [(z * 2 + c, ((z + shift) % 4) * 2 + c) for z in range(4) for c in range(2)]
    return lax.ppermute(item, "prompt", pairs)


def swap_cores(item):
    return lax.ppermute(item, "prompt", [(p, p ^ 1) for p in range(8)])


def spread(item, first):
    return [move_plane(item, s, first) if s else item for s in SHIFTS]


class Place:
    def __init__(self, source_of):
        here = lax.axis_index("prompt")
        spot = jnp.arange(source_of.shape[0], dtype=jnp.int32)
        mine = jnp.sum(jnp.where(spot == here, source_of, 0))
        other = jnp.sum(jnp.where(spot == (here ^ 1), source_of, 0))
        self.first = (here & 1) == 0
        self.steps = [((here >> 1) - (who >> 1)) & 3 for who in (mine, other)]
        self.same = [((who ^ here) & 1) == 0 for who in (mine, other)]

    def of(self, column, which):
        step = self.steps[which]
        low = jnp.where((step & 1) == 0, column[0], column[1])
        high = jnp.where((step & 1) == 0, column[2], column[3])
        return jnp.where(step < 2, low, high)


def tie(*trees):
    return lax.optimization_barrier(trees)


def bring_column(item):
    far, near, back = [move_z(item, s) for s in (2, 1, 3)]
    return [item, near, far, back]


def choose(column, place):
    mine, other = place.of(column, 0), place.of(column, 1)
    send = jnp.stack([jnp.where(place.first, p[1], p[0]) for p in (other, mine)])
    keep = jnp.stack([jnp.where(place.first, p[0], p[1]) for p in (mine, other)])
    return keep, send


def join(keep, got, place):
    return jnp.stack([jnp.where(place.same[i], keep[i], got[i]) for i in range(2)])


def bring_row(pair):
    return jnp.stack(spread(pair, True), axis=1)


def cross(kept):
    return swap_cores(jnp.stack([part[1] for part in kept]))


def return_row(keep, got):
    return [jnp.stack([keep[a], got[a]]) for a in range(SIDE)]


def move_back(items, first):
    return [move_plane(item, -s, first) if s else item for item, s in zip(items, SHIFTS)]


def add_up(items):
    return sum(item.astype(jnp.float32) for item in items).astype(jnp.bfloat16)


def give_back(row, place):
    pair = add_up(move_back([row[:, b] for b in range(SIDE)], True))
    column = bring_column(pair)

    def pick(which, same):
        both = place.of(column, which)
        return jnp.where(same, both[0], both[1])

    kept = pick(0, place.same[0])
    crossed = swap_cores(pick(1, place.same[1]))
    dk = jnp.where(place.first, kept, crossed)
    dv = jnp.where(place.first, crossed, kept)
    return dk.astype(jnp.float32)[None], dv.astype(jnp.float32)[None]


def body(prefix_k, prefix_v, queries, comp_k, comp_v, out_grad, lengths, owner_map):
    groups = jnp.arange(owner_map.shape[0], dtype=jnp.int32)
    holder = jnp.sum(jnp.where(owner_map[None, :] == groups[:, None], groups[None, :], 0), axis=1)
    rows_in = [queries[0], out_grad[0], comp_k[0], comp_v[0]]

    place = Place(holder)
    is_key = lax.broadcasted_iota(jnp.int32, (2, 1, 1), 0) == 0
    keep, send = choose(bring_column(jnp.where(is_key, prefix_k, prefix_v)), place)
    row = bring_row(join(keep, swap_cores(send), place))
    rows = [row[..., g[0] * HEAD_DIM : (g[-1] + 1) * HEAD_DIM] for g in GATHER_GROUPS]
    kept = spread(rows[0], False)
    kept, rest_row = tie(kept, rows[1])
    crossed = cross(kept)
    rest_kept = spread(rest_row, False)

    def call(group, kept, crossed, held):
        outs = attend(group, lengths, rows_in, kept, crossed, 0, 0, len(group), held, None)
        return list(outs[:4]), list(outs[4:])

    held, (keep, send) = call(GATHER_GROUPS[0], kept, crossed, None)
    send, rest_kept = tie(send, rest_kept)
    got = swap_cores(send)
    handed = jnp.stack([part[1] for part in rest_kept])
    handed, got = tie(handed, got)
    rest_crossed = swap_cores(handed)
    back = move_back(return_row(keep, got), False)
    held, (rest_keep, rest_send) = call(GATHER_GROUPS[1], rest_kept, rest_crossed, held)
    rest_send, back = tie(rest_send, back)
    rest_back = move_back(return_row(rest_keep, swap_cores(rest_send)), False)
    row = jnp.concatenate([add_up(back), add_up(rest_back)], axis=-1)
    grad_prefix_k, grad_prefix_v = give_back(row, Place(owner_map))
    attended, grad_queries, grad_comp_k, grad_comp_v = held
    return (
        attended[None],
        grad_queries[None],
        grad_comp_k[None],
        grad_comp_v[None],
        grad_prefix_k,
        grad_prefix_v,
    )


def solution(mesh):
    by_prompt = P("prompt", "learner", None)
    by_completion = P(("prompt", "learner"), None, None)
    return jax.shard_map(
        body,
        mesh=mesh,
        in_specs=(by_prompt,) * 2 + (by_completion,) * 4 + (P(), P()),
        out_specs=(by_completion,) * 4 + (by_prompt,) * 2,
        check_vma=False,
    )
```

```python
import functools

import jax
import jax.numpy as jnp
from jax import lax
from jax.experimental import pallas as pl
from jax.experimental.pallas import tpu as pltpu
from jax.sharding import PartitionSpec as P

KV_HEADS = 4
HEAD_DIM = 128
COMP_LEN = 256
Q_PER_KV = 5
SHARD = 128
SIDE = 4
PREFIX = SIDE * SIDE * SHARD
TOTAL = PREFIX + COMP_LEN

INV_ROOT = HEAD_DIM**-0.5
EXP2_SCALE = INV_ROOT * 1.4426950408889634
VERY_LOW = -1e30

SHIFTS = (0, 2, 1, 3)

GATHER_GROUPS = ((0, 1), (2, 3))

NN = (((1,), (0,)), ((), ()))
NT = (((1,), (1,)), ((), ()))


def mxu(left, right, dims):
    return lax.dot_general(left, right, dims, preferred_element_type=jnp.float32)


def attend_kernel(tile, n_alias, len_ref, q_ref, g_ref, ck_ref, cv_ref, *rest):
    kept, crossed = rest[0:4], rest[4]
    att_ref, dq_ref, dck_ref, dcv_ref, keep_ref, send_ref = rest[5 + n_alias : 11 + n_alias]
    keys, vals, acc_k, acc_v = rest[11 + n_alias :]
    here = lax.axis_index("prompt")
    core = here & 1
    length = len_ref[here * lax.axis_size("learner") + lax.axis_index("learner")]
    own = pl.ds(PREFIX, COMP_LEN)
    width = pl.ds(0, HEAD_DIM)
    spans = [pl.ds(t, tile) for t in range(0, PREFIX, tile)] + [own]

    def fill(mine, theirs):
        for a in range(SIDE):
            for b in range(SIDE):
                mine[pl.ds((a * SIDE + b) * SHARD, SHARD), width] = kept[a][0, b]
                theirs[pl.ds((b * SIDE + a) * SHARD, SHARD), width] = crossed[a, b]

    @pl.when(core == 0)
    def _():
        fill(keys, vals)

    @pl.when(core == 1)
    def _():
        fill(vals, keys)

    keys[own, :] = ck_ref[...]
    vals[own, width] = cv_ref[...]
    vals[:, pl.ds(HEAD_DIM, HEAD_DIM)] = jnp.ones((TOTAL, HEAD_DIM), jnp.bfloat16)
    row_no = lax.broadcasted_iota(jnp.int32, (COMP_LEN, COMP_LEN), 0)
    col_no = lax.broadcasted_iota(jnp.int32, (COMP_LEN, COMP_LEN), 1)
    visible = col_no <= row_no
    live = lax.broadcasted_iota(jnp.int32, (COMP_LEN, 1), 0) < length

    def forward(member):
        query = q_ref[:, pl.ds(member * HEAD_DIM, HEAD_DIM)]
        scores = [mxu(query, keys[span, :], NT) for span in spans]
        scores[-1] = jnp.where(visible, scores[-1], VERY_LOW)
        top = functools.reduce(jnp.maximum, [jnp.max(s, axis=1, keepdims=True) for s in scores])
        top = top * EXP2_SCALE
        grad = g_ref[:, pl.ds(member * HEAD_DIM, HEAD_DIM)]
        dweights = [mxu(grad, vals[span, width], NT) for span in spans]
        weights = [jnp.exp2(s * EXP2_SCALE - top) for s in scores]
        weights_bf = [w.astype(jnp.bfloat16) for w in weights]
        numer = sum(mxu(w, vals[span, :], NN) for w, span in zip(weights_bf, spans))
        numer, total = numer[:, :HEAD_DIM], numer[:, HEAD_DIM : HEAD_DIM + 1]
        return query, grad, dweights, weights, weights_bf, total, numer

    def backward(member, query, grad, dweights, weights, weights_bf, total, numer):
        cols = pl.ds(member * HEAD_DIM, HEAD_DIM)
        inv_total = jnp.where(live, 1.0 / total, 0.0)
        attended = (numer * inv_total).astype(jnp.bfloat16)
        att_ref[:, cols] = attended
        grad_wide = grad.astype(jnp.float32)
        dsum = jnp.sum(attended.astype(jnp.float32) * grad_wide, axis=1, keepdims=True)
        grad_t = (grad_wide * inv_total).astype(jnp.bfloat16).T
        query_t = (query.astype(jnp.float32) * (inv_total * INV_ROOT)).astype(jnp.bfloat16).T
        dq = 0.0
        for span, dweight, w, w_bf in zip(spans, dweights, weights, weights_bf):
            dscore = (w * (dweight - dsum)).astype(jnp.bfloat16)
            dq = dq + mxu(dscore, keys[span, :], NN)
            dk, dv = mxu(query_t, dscore, NN), mxu(grad_t, w_bf, NN)
            if member:
                acc_k[:, span] += dk
                acc_v[:, span] += dv
            else:
                acc_k[:, span] = dk
                acc_v[:, span] = dv
        dq_ref[:, cols] = (dq * (inv_total * INV_ROOT)).astype(jnp.bfloat16)

    done = forward(0)
    for member in range(Q_PER_KV):
        ahead = forward(member + 1) if member + 1 < Q_PER_KV else None
        backward(member, *done)
        done = ahead

    def empty(mine, theirs):
        for a in range(SIDE):
            for b in range(SIDE):
                cols = pl.ds((a * SIDE + b) * SHARD, SHARD)
                keep_ref[a, b] = mine[:, cols].T.astype(jnp.bfloat16)
                cols = pl.ds((b * SIDE + a) * SHARD, SHARD)
                send_ref[a, b] = theirs[:, cols].T.astype(jnp.bfloat16)

    @pl.when(core == 0)
    def _():
        empty(acc_k, acc_v)

    @pl.when(core == 1)
    def _():
        empty(acc_v, acc_k)

    dck_ref[...] = acc_k[:, own].T.astype(jnp.bfloat16)
    dcv_ref[...] = acc_v[:, own].T.astype(jnp.bfloat16)


def attend(heads, lengths, rows_in, kept, crossed, in_at, out_at, out_heads, held, grads):
    first = heads[0]
    per_head = pl.BlockSpec(
        (COMP_LEN, Q_PER_KV * HEAD_DIM), lambda h, _: (0, h + first)
    )
    per_kv = pl.BlockSpec((COMP_LEN, HEAD_DIM), lambda h, _: (0, h + first))
    kept_in = pl.BlockSpec((1, SIDE, SHARD, HEAD_DIM), lambda h, _: (0, 0, 0, h + in_at))
    square = (SIDE, SIDE, SHARD, HEAD_DIM)
    crossed_in = pl.BlockSpec(square, lambda h, _: (0, 0, 0, h + in_at))
    square_out = pl.BlockSpec(square, lambda h, _: (0, 0, 0, h + out_at))
    wide = jax.ShapeDtypeStruct((COMP_LEN, KV_HEADS * Q_PER_KV * HEAD_DIM), jnp.bfloat16)
    narrow = jax.ShapeDtypeStruct((COMP_LEN, KV_HEADS * HEAD_DIM), jnp.bfloat16)
    part = jax.ShapeDtypeStruct((SIDE, SIDE, SHARD, out_heads * HEAD_DIM), jnp.bfloat16)
    extra, aliases = [], {}
    base = 1 + 4 + 5
    for out_no, item in enumerate((held or [None] * 4) + (grads or [None] * 2)):
        if item is not None:
            aliases[base + len(extra)] = out_no
            extra.append(item)
    return pl.pallas_call(
        functools.partial(attend_kernel, 256, len(extra)),
        grid_spec=pltpu.PrefetchScalarGridSpec(
            num_scalar_prefetch=1,
            grid=(len(heads),),
            in_specs=[per_head, per_head, per_kv, per_kv]
            + [kept_in] * 4
            + [crossed_in]
            + [pl.BlockSpec(memory_space=pl.ANY)] * len(extra),
            out_specs=[per_head, per_head, per_kv, per_kv] + [square_out] * 2,
            scratch_shapes=[
                pltpu.VMEM((TOTAL, HEAD_DIM), jnp.bfloat16),
                pltpu.VMEM((TOTAL, 2 * HEAD_DIM), jnp.bfloat16),
            ]
            + [pltpu.VMEM((HEAD_DIM, TOTAL), jnp.float32)] * 2,
        ),
        out_shape=[wide, wide, narrow, narrow] + [part] * 2,
        input_output_aliases=aliases,
        compiler_params=pltpu.CompilerParams(vmem_limit_bytes=48 * 2**20),
        cost_estimate=pl.CostEstimate(
            flops=len(heads) * 6 * 2 * Q_PER_KV * COMP_LEN * TOTAL * HEAD_DIM,
            bytes_accessed=len(heads) * 5 * 2**20,
            transcendentals=len(heads) * Q_PER_KV * COMP_LEN * TOTAL,
        ),
    )(lengths, *rows_in, *kept, crossed, *extra)


def move_plane(item, shift, first):
    pairs = []
    for p in range(8):
        along_x = (p % 2 == 0) == first
        for x in range(SIDE):
            for y in range(SIDE):
                to_x = (x + shift) % SIDE if along_x else x
                to_y = y if along_x else (y + shift) % SIDE
                pairs.append(((p * SIDE + x) * SIDE + y, (p * SIDE + to_x) * SIDE + to_y))
    return lax.ppermute(item, ("prompt", "learner"), pairs)


def move_z(item, shift):
    pairs = [(z * 2 + c, ((z + shift) % 4) * 2 + c) for z in range(4) for c in range(2)]
    return lax.ppermute(item, "prompt", pairs)


def swap_cores(item):
    return lax.ppermute(item, "prompt", [(p, p ^ 1) for p in range(8)])


def spread(item, first):
    return [move_plane(item, s, first) if s else item for s in SHIFTS]


class Place:
    def __init__(self, source_of):
        here = lax.axis_index("prompt")
        spot = jnp.arange(source_of.shape[0], dtype=jnp.int32)
        mine = jnp.sum(jnp.where(spot == here, source_of, 0))
        other = jnp.sum(jnp.where(spot == (here ^ 1), source_of, 0))
        self.first = (here & 1) == 0
        self.steps = [((here >> 1) - (who >> 1)) & 3 for who in (mine, other)]
        self.same = [((who ^ here) & 1) == 0 for who in (mine, other)]

    def of(self, column, which):
        step = self.steps[which]
        low = jnp.where((step & 1) == 0, column[0], column[1])
        high = jnp.where((step & 1) == 0, column[2], column[3])
        return jnp.where(step < 2, low, high)


def tie(*trees):
    return lax.optimization_barrier(trees)


def bring_column(item):
    far, near, back = [move_z(item, s) for s in (2, 1, 3)]
    return [item, near, far, back]


def choose(column, place):
    mine, other = place.of(column, 0), place.of(column, 1)
    send = jnp.stack([jnp.where(place.first, p[1], p[0]) for p in (other, mine)])
    keep = jnp.stack([jnp.where(place.first, p[0], p[1]) for p in (mine, other)])
    return keep, send


def join(keep, got, place):
    return jnp.stack([jnp.where(place.same[i], keep[i], got[i]) for i in range(2)])


def bring_row(pair):
    return jnp.stack(spread(pair, True), axis=1)


def cross(kept):
    return swap_cores(jnp.stack([part[1] for part in kept]))


def return_row(keep, got):
    return [jnp.stack([keep[a], got[a]]) for a in range(SIDE)]


def move_back(items, first):
    return [move_plane(item, -s, first) if s else item for item, s in zip(items, SHIFTS)]


def add_up(items):
    return sum(item.astype(jnp.float32) for item in items).astype(jnp.bfloat16)


def give_back(row, place):
    pair = add_up(move_back([row[:, b] for b in range(SIDE)], True))
    column = bring_column(pair)

    def pick(which, same):
        both = place.of(column, which)
        return jnp.where(same, both[0], both[1])

    kept = pick(0, place.same[0])
    crossed = swap_cores(pick(1, place.same[1]))
    dk = jnp.where(place.first, kept, crossed)
    dv = jnp.where(place.first, crossed, kept)
    return dk.astype(jnp.float32)[None], dv.astype(jnp.float32)[None]


def body(prefix_k, prefix_v, queries, comp_k, comp_v, out_grad, lengths, owner_map):
    groups = jnp.arange(owner_map.shape[0], dtype=jnp.int32)
    holder = jnp.sum(jnp.where(owner_map[None, :] == groups[:, None], groups[None, :], 0), axis=1)
    rows_in = [queries[0], out_grad[0], comp_k[0], comp_v[0]]

    place = Place(holder)
    is_key = lax.broadcasted_iota(jnp.int32, (2, 1, 1), 0) == 0
    keep, send = choose(bring_column(jnp.where(is_key, prefix_k, prefix_v)), place)
    row = bring_row(join(keep, swap_cores(send), place))
    rows = [row[..., g[0] * HEAD_DIM : (g[-1] + 1) * HEAD_DIM] for g in GATHER_GROUPS]
    kept = spread(rows[0], False)
    kept, rest_row = tie(kept, rows[1])
    crossed = cross(kept)
    rest_kept = spread(rest_row, False)

    def call(group, kept, crossed, held):
        outs = attend(group, lengths, rows_in, kept, crossed, 0, 0, len(group), held, None)
        return list(outs[:4]), list(outs[4:])

    held, (keep, send) = call(GATHER_GROUPS[0], kept, crossed, None)
    send, rest_kept = tie(send, rest_kept)
    got = swap_cores(send)
    handed = jnp.stack([part[1] for part in rest_kept])
    handed, got = tie(handed, got)
    rest_crossed = swap_cores(handed)
    back = move_back(return_row(keep, got), False)
    held, (rest_keep, rest_send) = call(GATHER_GROUPS[1], rest_kept, rest_crossed, held)
    rest_send, back = tie(rest_send, back)
    rest_back = move_back(return_row(rest_keep, swap_cores(rest_send)), False)
    row = jnp.concatenate([add_up(back), add_up(rest_back)], axis=-1)
    grad_prefix_k, grad_prefix_v = give_back(row, Place(owner_map))
    attended, grad_queries, grad_comp_k, grad_comp_v = held
    return (
        attended[None],
        grad_queries[None],
        grad_comp_k[None],
        grad_comp_v[None],
        grad_prefix_k,
        grad_prefix_v,
    )


def solution(mesh):
    by_prompt = P("prompt", "learner", None)
    by_completion = P(("prompt", "learner"), None, None)
    return jax.shard_map(
        body,
        mesh=mesh,
        in_specs=(by_prompt,) * 2 + (by_completion,) * 4 + (P(), P()),
        out_specs=(by_completion,) * 4 + (by_prompt,) * 2,
        check_vma=False,
    )
```
